32 devices in a mesh: seq: 4 (over z), chan: 8 (over y, x, core).
Axes of the slice: x: 2, y: 2, z: 4, core: 2. Of those that a mesh axis runs over, the one named last changes fastest.
Arguments:
- resid: bfloat16 [8192, 4096], P('seq', 'chan'), may hold values from -1100 to 1100
- norm_gain: bfloat16 [4096], P('chan'), may hold values from 0.5 to 1.5
- feat_weight: bfloat16 [4096, 3, 4096], P(None, None, 'chan'), may hold values from -0.09375 to 0.09375
- short_filter: float32 [3, 3, 4096], P(None, None, 'chan'), may hold values from -3.5 to 3.5
- mr_filter: bfloat16 [128, 4096], P(None, 'chan'), may hold values from -0.5 to 0.5
- gates_lr: bfloat16 [8192, 2, 4096], P('seq', None, 'chan'), may hold values from -6 to 6
- decay_rate: float32 [16, 4096], P(None, 'chan'), may hold values from 2.4414063e-06 to 0.0333333333
- residue: float32 [16, 4096], P(None, 'chan'), may hold values from -1.5 to 1.5
- skip_gain: float32 [4096], P('chan'), may hold values from 0.5 to 1.5
Outputs:
- mixed: bfloat16 [8192, 4096], P('seq', 'chan')
The draws below stay inside these ranges and needn't reach their ends.
All inputs are finite; a program needn't handle non-finite values.
Results may differ from the reference program's by a relative error of at most 0.012.
Values may be sent and summed in bfloat16 or wider, within the bound.
No kernel may reach another device: no remote copies, remote signals or barrier semaphores. Data moves between devices by JAX's collectives and lax.ppermute only.
A program may use at most 128 MiB of HBM per device.

```python
import math
import jax
import jax.numpy as jnp
from jax import lax

D = 4096
SHORT = 3
MR_LEN = 128
MODES = 16
LENGTH = 8192


def draw_resid(key, part):
    key_base, key_column, key_line = jax.random.split(key, 3)
    position = jnp.arange(D, dtype=jnp.float32) / max(D - 1, 1)
    column_scale = 10.0 ** jax.random.uniform(key_column, (D,), jnp.float32) * 3.0 ** (0.5 * position)
    line_scale = 10.0 ** jax.random.uniform(key_line, (LENGTH, 1), jnp.float32)
    base_values = jnp.clip(jax.random.normal(key_base, (LENGTH, D), jnp.float32), -6.0, 6.0)
    return (base_values * line_scale * column_scale[None]).astype(jnp.bfloat16)


def draw_decay_rate(key, part):
    key_slow = jax.random.fold_in(key, 2)
    lowest = math.log(0.02 / LENGTH)
    highest = math.log(1.0 / 30.0)
    return jnp.exp(jax.random.uniform(key_slow, (MODES, D), jnp.float32, lowest, highest))


def levels(rng, dims, pieces, least, largest):
    loudness = 1.0
    for dim, shards_of in pieces:
        steps = jax.random.uniform(jax.random.fold_in(jax.random.fold_in(rng, 6), dim), (shards_of,), jnp.float32, least / len(pieces), largest / len(pieces))
        loudness = loudness * jnp.repeat(jnp.exp(steps), dims[dim] // shards_of).reshape((-1,) + (1,) * (len(dims) - 1 - dim))
    return loudness


def gaussian(own_key, shape, spread, bound, cuts=(), held_as=jnp.bfloat16):
    drawn = jax.random.normal(own_key, shape, jnp.float32) * spread
    if len(cuts) > 0:
        drawn = levels(own_key, shape, cuts, -0.22, 0.18) * drawn
    return jnp.clip(drawn, min=-bound, max=bound).astype(held_as)


def setup_inputs(seed: int = 0) -> dict:
    arg_keys = jax.random.split(jax.random.key(seed), 10)
    resid = draw_resid(jax.random.fold_in(arg_keys[9], 71), 0)
    norm_gain = jnp.clip(1.0 + 0.1 * jax.random.normal(arg_keys[1], (D,), jnp.float32), 0.5, 1.5).astype(jnp.bfloat16)
    feat_weight = gaussian(arg_keys[2], (D, 3, D), D ** -0.5, 0.09375, ((2, 8),))
    short_filter = gaussian(arg_keys[3], (SHORT, 3, D), 0.6, 3.5, ((2, 8),), jnp.float32)
    mr_filter = gaussian(arg_keys[4], (MR_LEN, D), MR_LEN ** -0.5, 0.5, ((1, 8),))
    gates_lr = gaussian(arg_keys[5], (LENGTH, 2, D), 1.0, 6.0, ((0, 4), (2, 8)))
    decay_rate = draw_decay_rate(jax.random.fold_in(arg_keys[9], 71), 0)
    residue = gaussian(arg_keys[7], (MODES, D), 0.25, 1.5, ((1, 8),), jnp.float32)
    skip_gain = jnp.clip(0.5 + 1.0 * jax.random.uniform(arg_keys[8], (D,), jnp.float32) ** levels(arg_keys[8], (D,), ((0, 8),), -0.2, 0.2), 0.5, 1.5)
    return dict(resid=resid, norm_gain=norm_gain, feat_weight=feat_weight, short_filter=short_filter, mr_filter=mr_filter, gates_lr=gates_lr, decay_rate=decay_rate, residue=residue, skip_gain=skip_gain)


def grouped_causal(signal, taps_of_group, extra):
    group_width = 64
    group_count = D // group_width
    padded_len = 2 * LENGTH

    def one_group(inputs):
        signal_part = inputs[0]
        taps = taps_of_group(inputs[1:])
        spectrum = jnp.fft.rfft(signal_part, n=padded_len, axis=0) * jnp.fft.rfft(taps, n=padded_len, axis=0)
        return jnp.fft.irfft(spectrum, n=padded_len, axis=0)[:LENGTH]
    stacked = (signal.reshape(LENGTH, group_count, group_width).transpose(1, 0, 2),) + tuple((item.reshape(item.shape[0], group_count, group_width).transpose(1, 0, 2) for item in extra))
    result = lax.map(one_group, stacked)
    return result.transpose(1, 0, 2).reshape(LENGTH, D)

def long_conv(signal, decays, residues):
    times = jnp.arange(LENGTH, dtype=jnp.float32)
    weighted = residues * jnp.sqrt(-jnp.expm1(-2.0 * decays))

    def make_taps(parts):
        decay_part, weight_part = parts
        return lax.optimization_barrier(jnp.sum(weight_part[:, None, :] * jnp.exp(-decay_part[:, None, :] * times[None, :, None]), axis=0))
    return grouped_causal(signal, make_taps, (decays, weighted))

def medium_conv(signal, taps):

    def make_taps(parts):
        return parts[0]
    return grouped_causal(signal, make_taps, (taps,))

def reference(resid, norm_gain, feat_weight, short_filter, mr_filter, gates_lr, decay_rate, residue, skip_gain):
    values = resid.astype(jnp.float32)
    mean_square = lax.optimization_barrier(jnp.mean(values * values, axis=1, keepdims=True))
    normed = (values * lax.rsqrt(mean_square + 1e-05) * norm_gain.astype(jnp.float32)[None]).astype(jnp.bfloat16)
    projected = jnp.dot(normed.astype(jnp.float32), feat_weight.reshape(D, 3 * D).astype(jnp.float32), precision=lax.Precision.HIGHEST, preferred_element_type=jnp.float32)
    projected = projected.astype(jnp.bfloat16).reshape(LENGTH, 3, D)
    padded = jnp.concatenate([jnp.zeros((SHORT - 1, 3, D), projected.dtype), projected], axis=0)
    featured = jnp.zeros((LENGTH, 3, D), jnp.float32)
    for tap_index in range(SHORT):
        start_row = SHORT - 1 - tap_index
        featured = featured + padded[start_row:start_row + LENGTH].astype(jnp.float32) * short_filter[tap_index][None]
    product = (featured[:, 1] * featured[:, 2]).astype(jnp.bfloat16)
    medium = medium_conv(product.astype(jnp.float32), mr_filter.astype(jnp.float32))
    mixed_mr = (featured[:, 0] * medium).astype(jnp.bfloat16)
    gates = gates_lr.astype(jnp.float32)
    long_input = (gates[:, 1] * mixed_mr.astype(jnp.float32)).astype(jnp.bfloat16)
    long_out = long_conv(long_input.astype(jnp.float32), decay_rate, residue)
    return (gates[:, 0] * (long_out + skip_gain[None] * long_input.astype(jnp.float32))).astype(jnp.bfloat16)
```

```python
import functools
import jax
import jax.numpy as jnp
import ml_dtypes
import numpy as np
from jax import lax
from jax.experimental import pallas as pl
from jax.experimental.pallas import tpu as pltpu
from jax.sharding import PartitionSpec as P

D = 4096
norm_epsilon = 1e-05
span = 128
run = 32
group = 8 * run
lanes = 128
rim = 8
grant = 56 << 20


def split_pair(value):
    high = value.astype(ml_dtypes.bfloat16)
    return high, (value - high.astype(np.float64)).astype(ml_dtypes.bfloat16)


def transforms():
    size = 2 * span
    angle = np.pi * (2.0 * np.arange(span)[:, None] + 1.0) * np.arange(size)[None] / size
    forward = np.concatenate([np.cos(angle), -np.sin(angle)], axis=0)
    inverse = np.concatenate([np.cos(angle).T, -np.sin(angle).T], axis=1)[span:] / span
    f_hi, f_lo = split_pair(forward)
    g_hi, g_lo = split_pair(inverse)
    return np.concatenate([f_hi, f_lo], axis=0), np.concatenate([g_hi, g_lo], axis=0)


def dot(a, b):
    return jnp.dot(a, b, preferred_element_type=jnp.float32)


def chunks_of(tokens):
    tail = group
    sizes, left = [], tokens - tail
    while left > 2 * group:
        sizes.append(2 * group)
        left -= 2 * group
    sizes.append(left)
    starts = [sum(sizes[:i]) for i in range(len(sizes))]
    return [(tokens - tail, tail)] + list(zip(starts, sizes))


def stat_rows_of(tokens, width):
    return -(-3 * (tokens // width) // 16) * 16


def prepare_kernel(chunks, resid_ref, gain_ref, *outs):
    tokens, width = resid_ref.shape
    ones = jnp.ones((8, width), jnp.bfloat16)
    gain = gain_ref[...].astype(jnp.float32)
    contract = (((1,), (1,)), ((), ()))
    count = tokens // width
    rows = []
    for k in range(count):
        values = resid_ref[k * width : (k + 1) * width, :].astype(jnp.float32)
        square = values * values
        high = square.astype(jnp.bfloat16)
        low = (square - high.astype(jnp.float32)).astype(jnp.bfloat16)
        total = lax.dot_general(ones, high, contract, preferred_element_type=jnp.float32)
        total = total + lax.dot_general(ones, low, contract, preferred_element_type=jnp.float32)
        rows.append(total[0:1])
    parts, rest = [], jnp.concatenate(rows, axis=0)
    for _ in range(3):
        part = rest.astype(jnp.bfloat16)
        rest = rest - part.astype(jnp.float32)
        parts.append(part.astype(jnp.float32))
    spare = stat_rows_of(tokens, width) - 3 * count
    if spare:
        parts.append(jnp.zeros((spare, width), jnp.float32))
    size = chunks[0][1]
    outs[0][size:, :] = jnp.concatenate(parts, axis=0).astype(jnp.bfloat16)
    for (start, size), out in zip(chunks, outs):
        values = resid_ref[start : start + size, :].astype(jnp.float32)
        out[0:size, :] = (values * gain).astype(jnp.bfloat16)


def prepare(resid, norm_gain, chunks):
    tokens, width = resid.shape
    shapes = []
    for i, (_, size) in enumerate(chunks):
        extra = stat_rows_of(tokens, width) if i == 0 else 0
        shapes.append(jax.ShapeDtypeStruct((size + extra, width), jnp.bfloat16))
    return pl.pallas_call(
        functools.partial(prepare_kernel, chunks),
        out_shape=shapes,
        compiler_params=pltpu.CompilerParams(vmem_limit_bytes=grant),
        name="prepare",
    )(resid, norm_gain[None])


def project(size, x_refs, order_ref, inv, w_hbm, w_ref, sems, total, put):
    depth = x_refs[0].shape[1]
    copies = []
    for b in range(len(x_refs)):
        at = pl.multiple_of(order_ref[b] * depth, depth)
        here = pl.ds(b * depth, depth)
        copies.append(pltpu.make_async_copy(w_hbm.at[:, pl.ds(at, depth), :], w_ref.at[:, here, :], sems.at[b]))
        copies[-1].start()
    for b, x_ref in enumerate(x_refs):
        copies[b].wait()
        for s in range(3):
            part = dot(x_ref[0:size, :], w_ref[s, b * depth : (b + 1) * depth, :])
            if b == 0:
                total[s, 0:size, :] = part
            elif b < len(x_refs) - 1:
                total[s, 0:size, :] += part
            else:
                put(s, ((total[s, 0:size, :] + part) * inv).astype(jnp.bfloat16))


def scale_of(inv_ref, start, size):
    width = inv_ref.shape[0]
    pieces, at = [], start
    while at < start + size:
        column, row = divmod(at, width)
        count = min(width - row, start + size - at)
        pieces.append(inv_ref[row : row + count, column : column + 1])
        at += count
    return pieces[0] if len(pieces) == 1 else jnp.concatenate(pieces, axis=0)


def featured(pad, filt_ref, s, first, count):
    at = rim + first
    out = pad[s, at : at + count, :] * filt_ref[0, s : s + 1, :]
    for j in (1, 2):
        out = out + pad[s, at - j : at - j + count, :] * filt_ref[j, s : s + 1, :]
    return out


def first_kernel(blocks, start, tokens, *refs):
    x_refs, refs = refs[:blocks], refs[blocks:]
    order_ref, w_hbm, filt_ref, rows_ref, rim_ref, prod_ref, inv_ref, w_ref, pad, total, sems = refs
    size, width = rows_ref.shape[1], inv_ref.shape[0]
    count = tokens // width
    sums = jnp.zeros((count, width), jnp.float32)
    for part in range(3):
        for x_ref in x_refs:
            stats = x_ref[size:, :].astype(jnp.float32)
            sums = sums + stats[part * count : (part + 1) * count]
    inverse = lax.rsqrt(sums / D + norm_epsilon)
    if count < 8:
        inverse = jnp.concatenate([inverse, jnp.zeros((8 - count, width), jnp.float32)], axis=0)
    inv_ref[...] = inverse.T

    def put(s, value):
        rows_ref[s] = value
        pad[s, rim : rim + size, :] = value.astype(jnp.float32)

    project(size, x_refs, order_ref, scale_of(inv_ref, start, size), w_hbm, w_ref, sems, total, put)
    for s in range(3):
        rim_ref[s] = pad[s, size : size + rim, :]
    at = size - span
    prod_ref[...] = (featured(pad, filt_ref, 1, at, span) * featured(pad, filt_ref, 2, at, span)).astype(jnp.bfloat16)


def params():
    return pltpu.CompilerParams(vmem_limit_bytes=grant)


in_vmem = pl.BlockSpec(memory_space=pltpu.VMEM)
in_smem = pl.BlockSpec(memory_space=pltpu.SMEM)
in_hbm = pl.BlockSpec(memory_space=pl.ANY)


def weight_scratch(w, size):
    _, depth, width = w.shape
    return [
        pltpu.VMEM(w.shape, jnp.bfloat16),
        pltpu.VMEM((3, rim + size, width), jnp.float32),
        pltpu.VMEM((3, size, width), jnp.float32),
    ]


def project_first(blocks, order, w, filt, start, size, tokens):
    width = w.shape[2]
    return pl.pallas_call(
        functools.partial(first_kernel, len(blocks), start, tokens),
        in_specs=[in_vmem] * len(blocks) + [in_smem, in_hbm, in_vmem],
        out_specs=[in_vmem] * 4,
        out_shape=[
            jax.ShapeDtypeStruct((3, size, width), jnp.bfloat16),
            jax.ShapeDtypeStruct((3, rim, width), jnp.float32),
            jax.ShapeDtypeStruct((span, width), jnp.bfloat16),
            jax.ShapeDtypeStruct((width, 8), jnp.float32),
        ],
        scratch_shapes=weight_scratch(w, size) + [pltpu.SemaphoreType.DMA((len(blocks),))],
        compiler_params=params(),
        name="project_first",
    )(*blocks, order, w, filt)


def medium_block(window, f_ref, g_ref, spectrum_ref):
    both = dot(f_ref[...], window)
    spec = both[: 2 * span] + both[2 * span :]
    real, imag = spec[:span], spec[span:]
    h_real, h_imag = spectrum_ref[0], spectrum_ref[1]
    out = jnp.concatenate([real * h_real - imag * h_imag, real * h_imag + imag * h_real], axis=0)
    high = out.astype(jnp.bfloat16)
    low = (out - high.astype(jnp.float32)).astype(jnp.bfloat16)
    pair = dot(g_ref[...], high)
    return pair[:span] + pair[span:] + dot(g_ref[0:span, :], low)


def add_up(terms):
    while len(terms) > 1:
        paired = [terms[i] + terms[i + 1] for i in range(0, len(terms) - 1, 2)]
        terms = paired + terms[len(terms) - len(terms) % 2 :]
    return terms[0]


def recur(base, lane, u_ref, y_ref, a_ref, w_ref, skip_ref):
    modes = a_ref.shape[0]
    cols = pl.ds(lane * lanes, lanes)
    a = [a_ref[n, :, cols] for n in range(modes)]
    w = [w_ref[n, :, cols] for n in range(modes)]
    skip = skip_ref[:, cols]

    def step(t, state):
        at = pl.ds(base + t, 8, stride=run)
        u = u_ref[lane, at, :]
        state = tuple(s * d + u for s, d in zip(state, a))
        y_ref[lane, at, :] = add_up([s * v for s, v in zip(state, w)] + [skip * u])
        return state

    start = tuple(jnp.zeros((8, lanes), jnp.float32) for _ in range(modes))
    return lax.fori_loop(0, run, step, start, unroll=8)


def chain(state, lane, carry_ref, starts_ref, steps_ref, last):
    cols = pl.ds(lane * lanes, lanes)
    head = lax.broadcasted_iota(jnp.int32, (8, lanes), 0) == 0
    for n, end in enumerate(state):
        carry = carry_ref[n, :, cols]
        total = end + steps_ref[0, n, :, cols] * carry
        for k, by in enumerate((1, 2, 4)):
            total = total + steps_ref[k + 1, n, :, cols] * pltpu.roll(total, by, 0)
        starts_ref[n, :, cols] = jnp.where(head, carry, pltpu.roll(total, 1, 0))
        last[n, :, cols] = jnp.broadcast_to(total[7:8], (8, lanes))


def chunk_kernel(blocks, start, size, behind, *refs):
    x_refs, refs = refs[:blocks], refs[blocks:]
    order_ref, w_hbm, filt_ref, inv_ref, rows_in, prod_in, carry_in = refs[:7]
    refs = refs[7:]
    if behind:
        more_ref, refs = refs[0], refs[1:]
    gates_ref, f_ref, g_ref, spectrum_ref, a_ref, mode_ref, skip_ref, steps_ref = refs[:8]
    y_ref, starts_ref, rows_out, prod_out, carry_out, w_ref, pad, total, z_ref, u_ref, sems = refs[8:]
    count = size + behind

    def put(s, value):
        pad[s, rim : rim + size, :] = value.astype(jnp.float32)

    for s in range(3):
        pad[s, 0:rim, :] = rows_in[s]
        if behind:
            pad[s, rim + size : rim + count, :] = more_ref[s].astype(jnp.float32)
    project(size, x_refs, order_ref, scale_of(inv_ref, start, size), w_hbm, w_ref, sems, total, put)
    for s in range(3):
        rows_out[s] = pad[s, count : count + rim, :]
    z_ref[0:span, :] = prod_in[...]
    for b in range(count // span):
        first = b * span
        product = featured(pad, filt_ref, 1, first, span) * featured(pad, filt_ref, 2, first, span)
        z_ref[span + first : 2 * span + first, :] = product.astype(jnp.bfloat16)
    prod_out[...] = z_ref[count : count + span, :]
    groups = y_ref.shape[0]
    for b in range(count // span):
        first = b * span
        medium = medium_block(z_ref[first : first + 2 * span, :], f_ref, g_ref, spectrum_ref)
        mixed = (featured(pad, filt_ref, 0, first, span) * medium).astype(jnp.bfloat16)
        gate = gates_ref[first : first + span, 1, :].astype(jnp.float32)
        u = (gate * mixed.astype(jnp.float32)).astype(jnp.bfloat16).astype(jnp.float32)
        for lane in range(groups):
            u_ref[lane, first : first + span, :] = u[:, lane * lanes : (lane + 1) * lanes]
    for k in range(count // group):
        for lane in range(groups):
            state = recur(k * group, lane, u_ref, y_ref, a_ref, mode_ref, skip_ref)
            chain(state, lane, carry_in if k == 0 else carry_out, starts_ref.at[k], steps_ref, carry_out)


def whole(shape):
    return pl.BlockSpec(shape, lambda i: (0,) * len(shape))


def project_chunk(blocks, order, w, filt, inv, rows, prod, carry, more, gates, tables, start, size):
    width = w.shape[2]
    behind = 0 if more is None else more.shape[1]
    count = size + behind
    modes = carry.shape[0]
    small = [filt, inv, rows, prod, carry] + ([] if more is None else [more])
    outs = [
        jax.ShapeDtypeStruct((width // lanes, count, lanes), jnp.float32),
        jax.ShapeDtypeStruct((count // group, modes, 8, width), jnp.float32),
        jax.ShapeDtypeStruct((3, rim, width), jnp.float32),
        jax.ShapeDtypeStruct((span, width), jnp.bfloat16),
        jax.ShapeDtypeStruct((modes, 8, width), jnp.float32),
    ]
    return pl.pallas_call(
        functools.partial(chunk_kernel, len(blocks), start, size, behind),
        grid=(1,),
        in_specs=[whole(b.shape) for b in blocks]
        + [in_smem, in_hbm]
        + [whole(v.shape) for v in small]
        + [pl.BlockSpec((count, 2, width), lambda i: (start // count, 0, 0))]
        + [whole(v.shape) for v in tables],
        out_specs=[whole(o.shape) for o in outs],
        out_shape=outs,
        scratch_shapes=weight_scratch(w, count)
        + [
            pltpu.VMEM((span + count, width), jnp.bfloat16),
            pltpu.VMEM((width // lanes, count, lanes), jnp.float32),
            pltpu.SemaphoreType.DMA((len(blocks),)),
        ],
        compiler_params=params(),
        name="project_chunk",
    )(*blocks, order, w, *small, gates, *tables)


def finish_kernel(peers, counts, *refs):
    recv, refs = refs[:peers], refs[peers:]
    y_refs, refs = refs[: len(counts)], refs[len(counts) :]
    s_refs, refs = refs[: len(counts)], refs[len(counts) :]
    gates_ref, a_ref, mode_ref, skip_runs, skip_group, skip_block, out_ref, gate_buf, out_buf, incoming = refs
    step_index = pl.program_id(0)
    modes = a_ref.shape[0]
    groups = y_refs[0].shape[0]

    @pl.when(step_index == 0)
    def _():
        for n in range(modes):
            total = jnp.zeros((1, out_ref.shape[1]), jnp.float32)
            for k in range(peers):
                total = total + skip_block[k, n : n + 1, :] * recv[k][n : n + 1, :]
            incoming[n] = jnp.broadcast_to(total, (8, out_ref.shape[1]))

    gate = gates_ref[:, 0, :].astype(jnp.float32)
    for lane in range(groups):
        gate_buf[lane] = gate[:, lane * lanes : (lane + 1) * lanes]

    def one(y_ref, s_ref):
        for lane in range(groups):
            cols = pl.ds(lane * lanes, lanes)
            a = [a_ref[n, :, cols] for n in range(modes)]
            state = []
            for n in range(modes):
                coming = incoming[n, :, cols]
                state.append(mode_ref[n, :, cols] * a[n] * (s_ref[0, n, :, cols] + skip_runs[n, :, cols] * coming))
                incoming[n, :, cols] = coming * skip_group[n, :, cols]

            def step(t, state):
                at = pl.ds(t, 8, stride=run)
                y = add_up(list(state) + [y_ref[lane, at, :]])
                out_buf[lane, at, :] = y * gate_buf[lane, at, :]
                return tuple(s * d for s, d in zip(state, a))

            lax.fori_loop(0, run, step, tuple(state), unroll=8)
            out_ref[:, lane * lanes : (lane + 1) * lanes] = out_buf[lane].astype(jnp.bfloat16)

    first = 0
    for k, count in enumerate(counts):
        @pl.when(jnp.logical_and(step_index >= first, step_index < first + count))
        def _(k=k):
            one(y_refs[k], s_refs[k])
        first += count


def finish(recv, ys, starts, gates, tables, tokens):
    width = gates.shape[2]
    counts = [s.shape[0] for s in starts]
    firsts = [sum(counts[:i]) for i in range(len(counts))]
    modes = starts[0].shape[1]
    place = lambda i, k: jnp.clip(i - firsts[k], 0, counts[k] - 1)
    return pl.pallas_call(
        functools.partial(finish_kernel, len(recv), counts),
        grid=(tokens // group,),
        in_specs=[whole(r.shape) for r in recv]
        + [pl.BlockSpec((width // lanes, group, lanes), lambda i, k=k: (0, place(i, k), 0)) for k in range(len(counts))]
        + [pl.BlockSpec((1, modes, 8, width), lambda i, k=k: (place(i, k), 0, 0, 0)) for k in range(len(counts))]
        + [pl.BlockSpec((group, 2, width), lambda i: (i, 0, 0))]
        + [whole(t.shape) for t in tables],
        out_specs=pl.BlockSpec((group, width), lambda i: (i, 0)),
        out_shape=jax.ShapeDtypeStruct((tokens, width), jnp.bfloat16),
        scratch_shapes=[
            pltpu.VMEM((width // lanes, group, lanes), jnp.float32),
            pltpu.VMEM((width // lanes, group, lanes), jnp.float32),
            pltpu.VMEM((modes, 8, width), jnp.float32),
        ],
        compiler_params=params(),
        name="finish",
    )(*recv, *ys, *starts, gates, *tables)


def flipped(value, mask):
    peers = lax.axis_size("chan")
    return lax.ppermute(value, "chan", [(i, i ^ mask) for i in range(peers)])


def shifted(value, by):
    peers = lax.axis_size("seq")
    return lax.ppermute(value, "seq", [(i, i + by) for i in range(peers - by)])


def gather(own, index):
    peers = lax.axis_size("chan")
    if peers != 8:
        every = lax.all_gather(own, "chan")
        return [every[i] for i in range(peers)]
    x, y = flipped(own, 2), flipped(own, 4)
    far = flipped(x, 4) if index % 2 else flipped(y, 2)
    blocks = []
    for block in (own, x, y, far):
        blocks += [block, flipped(block, 1)]
    return blocks


def on_device(
    resid, norm_gain, feat_weight, short_filter, mr_filter, gates_lr, decay_rate, residue, skip_gain
):
    tokens, width = resid.shape
    modes = decay_rate.shape[0]
    chunks = chunks_of(tokens)
    peers = lax.axis_size("chan")
    me = lax.axis_index("chan")
    order = jnp.arange(peers, dtype=jnp.int32)
    if peers == 8:
        order = me ^ order
    weight = feat_weight.transpose(1, 0, 2)
    forward, inverse = (jnp.asarray(t) for t in transforms())
    taps = mr_filter.astype(jnp.bfloat16)
    spectrum = dot(forward[:, : taps.shape[0]], taps)
    spectrum = (spectrum[: 2 * span] + spectrum[2 * span :]).reshape(2, span, width)

    def rows8(value):
        return jnp.broadcast_to(value[:, None], (modes, 8, width))

    def decayed(by):
        return jnp.exp(-decay_rate * by)

    runs = jnp.arange(8, dtype=jnp.float32)[None, :, None]
    steps = [jnp.where(runs == 0, decayed(run)[:, None], 0.0)]
    steps += [jnp.where(runs >= by, decayed(run * by)[:, None], 0.0) for by in (1, 2, 4)]
    weighted = residue * jnp.sqrt(-jnp.expm1(-2.0 * decay_rate))
    decays, weights = rows8(decayed(1.0)), rows8(weighted)
    skip = jnp.broadcast_to(skip_gain[None], (8, width))
    tables = [forward, inverse, spectrum, decays, weights, skip, jnp.stack(steps)]

    sent = prepare(resid, norm_gain, chunks)
    blocks = [gather(own, i) for i, own in enumerate(sent)]
    (start, size), later = chunks[0], chunks[1:]
    more, rows, prod, inv = project_first(blocks[0], order, weight, short_filter, start, size, tokens)
    rows, prod = shifted(rows, 1), shifted(prod, 1)
    carry = jnp.zeros((modes, 8, width), jnp.float32)
    ys, starts = [], []
    for i, (start, size) in enumerate(later):
        y, s, rows, prod, carry = project_chunk(
            blocks[i + 1], order, weight, short_filter, inv, rows, prod, carry,
            more if i == len(later) - 1 else None, gates_lr, tables, start, size,
        )
        ys.append(y)
        starts.append(s)
    seq_peers = lax.axis_size("seq")
    end = carry[:, 0, :]
    recv = [shifted(end, by) for by in range(1, seq_peers)]
    block_steps = jnp.stack([decayed(float(tokens * k)) for k in range(seq_peers - 1)])
    run_steps = jnp.exp(-decay_rate[:, None] * (run * runs))
    finish_tables = [decays, weights, run_steps, rows8(decayed(group)), block_steps]
    return finish(recv, ys, starts, gates_lr, finish_tables, tokens)


def solution(mesh):
    in_specs = (
        P("seq", "chan"),
        P("chan"),
        P(None, None, "chan"),
        P(None, None, "chan"),
        P(None, "chan"),
        P("seq", None, "chan"),
        P(None, "chan"),
        P(None, "chan"),
        P("chan"),
    )
    out_specs = P("seq", "chan")
    return jax.shard_map(
        on_device, mesh=mesh, in_specs=in_specs, out_specs=out_specs, check_vma=False
    )
```

```python
import functools
import math
import jax
import jax.numpy as jnp
import ml_dtypes
import numpy as np
from jax import lax
from jax.experimental import pallas as pl
from jax.experimental.pallas import tpu as pltpu
from jax.sharding import PartitionSpec as P

D = 4096
norm_epsilon = 1e-05
span = 128
run = span // 8
tail_rows = 256
lanes = 128
rim = 16


def split_pair(value):
    high = value.astype(ml_dtypes.bfloat16)
    return high, (value - high.astype(np.float64)).astype(ml_dtypes.bfloat16)


def token_of_row():
    row = np.arange(span)
    return run * (row % 8) + row // 8


def shuffle():
    return np.eye(span)[token_of_row()].astype(ml_dtypes.bfloat16)


def transforms():
    size = 2 * span
    order = token_of_row()
    times = np.concatenate([order, span + order])
    angle = np.pi * (2.0 * np.arange(span)[:, None] + 1.0) * times[None] / size
    forward = np.concatenate([np.cos(angle), -np.sin(angle)], axis=0)
    inverse = np.concatenate([np.cos(angle).T, -np.sin(angle).T], axis=1)[span:] / span
    f_hi, f_lo = split_pair(forward)
    g_hi, g_lo = split_pair(inverse)
    return np.concatenate([f_hi, f_lo], axis=0), np.concatenate([g_hi, g_lo], axis=0)


def dot(a, b):
    return jnp.dot(a, b, preferred_element_type=jnp.float32)


def parts_of(tokens):
    tail, first = 2 * span, 3 * span
    rest = tokens - tail - first
    second = -(-rest // (2 * span)) * span
    return [
        [(tokens - tail, tail), (0, first)],
        [(first, second)],
        [(first + second, rest - second)],
    ]


def rows_of(part):
    return sum(size for _, size in part)


def stat_rows_of(tokens, width):
    return -(-3 * (tokens // width) // 16) * 16


def prepare_kernel(parts, resid_ref, gain_ref, shuffle_ref, all_ref, *outs):
    tokens, width = resid_ref.shape
    ones = jnp.ones((8, width), jnp.bfloat16)
    gain = gain_ref[...].astype(jnp.float32)
    contract = (((1,), (1,)), ((), ()))
    sums = []
    base = 0
    for out, part in zip(outs, parts):
        here = 0
        for start, size in part:
            for at in range(start, start + size, span):
                values = dot(shuffle_ref[...], resid_ref[at : at + span, :])
                scaled = (values * gain).astype(jnp.bfloat16)
                out[here : here + span, :] = scaled
                all_ref[base + here : base + here + span, :] = scaled
                here += span
                square = values * values
                high = square.astype(jnp.bfloat16)
                low = (square - high.astype(jnp.float32)).astype(jnp.bfloat16)
                total = lax.dot_general(ones, high, contract, preferred_element_type=jnp.float32)
                total = total + lax.dot_general(ones, low, contract, preferred_element_type=jnp.float32)
                sums.append((at, total[0:1]))
        base += out.shape[0]
    sums = jnp.concatenate([total for _, total in sorted(sums, key=lambda pair: pair[0])], axis=1)
    count = tokens // width
    rest = jnp.concatenate([sums[:, k * width : (k + 1) * width] for k in range(count)], axis=0)
    shares = []
    for _ in range(3):
        share = rest.astype(jnp.bfloat16)
        rest = rest - share.astype(jnp.float32)
        shares.append(share.astype(jnp.float32))
    spare = stat_rows_of(tokens, width) - 3 * count
    if spare:
        shares.append(jnp.zeros((spare, width), jnp.float32))
    stats = jnp.concatenate(shares, axis=0).astype(jnp.bfloat16)
    first = rows_of(parts[0])
    outs[0][first:, :] = stats
    all_ref[first : first + stats.shape[0], :] = stats


def prepare(resid, norm_gain, shuffler, parts):
    tokens, width = resid.shape
    extra = stat_rows_of(tokens, width)
    shapes = [jax.ShapeDtypeStruct((tokens + extra, width), jnp.bfloat16)]
    for i, part in enumerate(parts):
        shapes.append(jax.ShapeDtypeStruct((rows_of(part) + (extra if i == 0 else 0), width), jnp.bfloat16))
    return pl.pallas_call(
        functools.partial(prepare_kernel, parts),
        out_shape=shapes,
        compiler_params=params([resid, shuffler], shapes),
        name="prepare",
    )(resid, norm_gain[None], shuffler)


def gates_kernel(spans, gates_ref, select_ref, out_ref, *in_refs):
    width = out_ref.shape[1]
    for in_ref, first in zip(in_refs, spans):
        for k in range(in_ref.shape[0] // span):
            at = first + k * span
            both = dot(select_ref[...], gates_ref[at : at + span].reshape(2 * span, width))
            out_ref[at : at + span, :] = both[:span].astype(jnp.bfloat16)
            in_ref[k * span : (k + 1) * span, :] = both[span:].astype(jnp.bfloat16)


def shuffle_gates(gates, spans, sizes):
    tokens, _, width = gates.shape
    select = np.zeros((2 * span, 2 * span), np.float32)
    for row, token in enumerate(token_of_row()):
        select[row, 2 * token] = 1.0
        select[span + row, 2 * token + 1] = 1.0
    outs = [jax.ShapeDtypeStruct((size, width), jnp.bfloat16) for size in [tokens, *sizes]]
    return pl.pallas_call(
        functools.partial(gates_kernel, spans),
        in_specs=[in_vmem] * 2,
        out_specs=[in_vmem] * (1 + len(sizes)),
        out_shape=outs,
        compiler_params=params([gates], outs),
        name="shuffle_gates",
    )(gates, jnp.asarray(select, jnp.bfloat16))


def project_steps(size, pieces, order_ref, w_ref, total, begun=None):
    def one(b, s, ref, src, dst, rows):
        depth = ref.shape[1]
        at = pl.multiple_of(order_ref[b] * depth, depth)
        here = slice(dst, dst + rows)
        part = dot(ref[src : src + rows, :], w_ref[s, pl.ds(at, depth), :])
        if b == 0 and begun is None:
            total[s, here, :] = part
        elif b == 2 and begun is not None:
            total[s, here, :] = begun[s, here, :] + part
        else:
            total[s, here, :] += part

    steps = []
    for b, parts in enumerate(pieces):
        for s in range(3):
            for ref, src, dst, rows in parts:
                steps.append(functools.partial(one, b, s, ref, src, dst, min(rows, size - dst)))
    return steps if begun is None else [step for step in steps if step.args[0] >= 2]


def begin(every, twin, order, w, bases, sizes):
    width = w.shape[2]

    def kernel(own_ref, twin_ref, order_ref, w_ref, *outs):
        for out, base, size in zip(outs, bases, sizes):
            pieces = [[(own_ref, base, 0, size)], [(twin_ref, base, 0, size)]]
            for step in project_steps(size, pieces, order_ref, w_ref, out):
                step()

    outs = [jax.ShapeDtypeStruct((3, size, width), jnp.float32) for size in sizes]
    return pl.pallas_call(
        kernel,
        in_specs=[in_vmem] * 2 + [in_smem, in_vmem],
        out_specs=[in_vmem] * len(sizes),
        out_shape=outs,
        compiler_params=params([every, twin, w], outs),
        name="begin",
    )(every, twin, order, w)


def bind(layout, refs):
    return [[(refs[i], src, dst, rows) for i, src, dst, rows in parts] for parts in layout]


def params(operands, outs, scratch=()):
    held = sum(math.prod(a.shape) * a.dtype.itemsize for a in (*operands, *outs))
    held += sum(math.prod(a.shape) * jnp.dtype(a.dtype).itemsize for a in scratch if len(a.shape) > 1)
    return pltpu.CompilerParams(vmem_limit_bytes=held + (3 << 20))


def whole(shape):
    return pl.BlockSpec(shape, lambda i: (0,) * len(shape))


in_vmem = pl.BlockSpec(memory_space=pltpu.VMEM)
in_smem = pl.BlockSpec(memory_space=pltpu.SMEM)
in_hbm = pl.BlockSpec(memory_space=pl.ANY)

def scale_of(inv_ref, start, size):
    width = inv_ref.shape[0]
    pieces, at = [], start
    while at < start + size:
        column, row = divmod(at, width)
        count = min(width - row, start + size - at)
        pieces.append(inv_ref[row : row + count, column : column + 1])
        at += count
    return pieces[0] if len(pieces) == 1 else jnp.concatenate(pieces, axis=0)


def lead_in(s, k, pad, before):
    base = k * (rim + span)
    head = lax.broadcasted_iota(jnp.int32, (8, pad.shape[2]), 0) == 0
    for half in range(2):
        last = pad[s, base + span + 8 * half : base + span + 8 * half + 8, :]
        pad[s, base + 8 * half : base + 8 * half + 8, :] = jnp.where(head, pltpu.roll(before[half], 1, 0), pltpu.roll(last, 1, 0))


def lead_in_all(s, count, pad, rim_ref):
    last = rim_ref[s * rim : (s + 1) * rim, :].astype(jnp.float32)
    before = [last[0:8], last[8:16]]
    for k in range(count // span):
        lead_in(s, k, pad, before)
        end = (k + 1) * (rim + span)
        before = [pad[s, end - 16 : end - 8, :], pad[s, end - 8 : end, :]]


def place_rows(s, first, value, pad):
    for k in range(value.shape[0] // span):
        base = (first // span + k) * (rim + span) + rim
        pad[s, base : base + span, :] = value[k * span : (k + 1) * span].astype(jnp.float32)


def featured(pad, filt_ref, s, k):
    base = k * (rim + span)
    out = pad[s, base + 16 : base + 16 + span, :] * filt_ref[0, s : s + 1, :]
    out = out + pad[s, base + 8 : base + 8 + span, :] * filt_ref[1, s : s + 1, :]
    return out + pad[s, base : base + span, :] * filt_ref[2, s : s + 1, :]


def first_kernel(layout, count_x, part, tokens, *refs):
    x_refs, refs = refs[:count_x], refs[count_x:]
    order_ref, w_ref, begun, filt_ref, tail_ref, rows_ref, rim_ref, inv_ref, pad, total = refs
    size, tail, width = rows_of(part), tail_ref.shape[1], inv_ref.shape[0]
    pieces = bind(layout, x_refs)
    count = tokens // width
    stat_count = stat_rows_of(tokens, width)
    sums = jnp.zeros((count, width), jnp.float32)
    for parts in pieces:
        ref, src, dst, rows = parts[-1]
        stats = ref[src + size - dst : src + size - dst + stat_count, :].astype(jnp.float32)
        for k in range(3):
            sums = sums + stats[k * count : (k + 1) * count]
    inverse = lax.rsqrt(sums / D + norm_epsilon)
    if count < 8:
        inverse = jnp.concatenate([inverse, jnp.zeros((8 - count, width), jnp.float32)], axis=0)
    inv_ref[...] = inverse.T
    for step in project_steps(size, pieces, order_ref, w_ref, total, begun):
        step()
    end = (tail // span) * (rim + span)
    for s in range(3):
        tail_ref[s] = (total[s, 0:tail, :] * scale_of(inv_ref, *part[0])).astype(jnp.bfloat16)
        rows_ref[s] = (total[s, tail:, :] * scale_of(inv_ref, *part[1])).astype(jnp.bfloat16)
        place_rows(s, 0, tail_ref[s], pad)
        rim_ref[s * rim : (s + 1) * rim, :] = tail_ref[s, tail - rim :, :]
        lead_in_all(s, tail, pad, rim_ref)
    last = tail // span - 1
    product = featured(pad, filt_ref, 1, last) * featured(pad, filt_ref, 2, last)
    rim_ref[3 * rim :, :] = product.astype(jnp.bfloat16)


def project_first(gathered, order, w, begun, filt, part, tokens):
    layout, arrays = gathered
    width = w.shape[2]
    (_, tail), (_, size) = part
    operands = [*arrays, order, w, begun, filt]
    outs = [
        jax.ShapeDtypeStruct((3, tail, width), jnp.bfloat16),
        jax.ShapeDtypeStruct((3, size, width), jnp.bfloat16),
        jax.ShapeDtypeStruct((3 * rim + span, width), jnp.bfloat16),
        jax.ShapeDtypeStruct((width, 8), jnp.float32),
    ]
    scratch = [
        pltpu.VMEM((3, groups_rows(tail), width), jnp.float32),
        pltpu.VMEM((3, tail + size, width), jnp.float32),
    ]
    return pl.pallas_call(
        functools.partial(first_kernel, layout, len(arrays), part, tokens),
        in_specs=[in_vmem] * len(arrays) + [in_smem] + [in_vmem] * 3,
        out_specs=[in_vmem] * 4,
        out_shape=outs,
        scratch_shapes=scratch,
        compiler_params=params(operands, outs, scratch),
        name="project_first",
    )(*operands)


def medium_block(window, f_ref, g_ref, spectrum_ref):
    both = dot(f_ref[...], window)
    spec = both[: 2 * span] + both[2 * span :]
    real, imag = spec[:span], spec[span:]
    h_real, h_imag = spectrum_ref[0], spectrum_ref[1]
    out = jnp.concatenate([real * h_real - imag * h_imag, real * h_imag + imag * h_real], axis=0)
    high = out.astype(jnp.bfloat16)
    low = (out - high.astype(jnp.float32)).astype(jnp.bfloat16)
    pair = dot(g_ref[...], high)
    return pair[:span] + pair[span:] + dot(g_ref[0:span, :], low)


def add_up(terms):
    while len(terms) > 1:
        paired = [terms[i] + terms[i + 1] for i in range(0, len(terms) - 1, 2)]
        terms = paired + terms[len(terms) - len(terms) % 2 :]
    return terms[0]


def recur(k, cols, u_ref, y_ref, a_ref, w_ref, skip_ref):
    modes = a_ref.shape[0]
    a = [a_ref[n, :, cols] for n in range(modes)]
    w = [w_ref[n, :, cols] for n in range(modes)]
    skip = skip_ref[:, cols]
    state = [None] * modes
    for t in range(run):
        rows = slice(k * span + 8 * t, k * span + 8 * t + 8)
        u = u_ref[rows, cols]
        state = [u if t == 0 else s * d + u for s, d in zip(state, a)]
        y_ref[rows, cols] = add_up([s * v for s, v in zip(state, w)] + [skip * u])
    return state


def chain(state, cols, carry_ref, starts_ref, steps_ref, last):
    head = lax.broadcasted_iota(jnp.int32, (8, lanes), 0) == 0
    for n, end in enumerate(state):
        carry = carry_ref[n, :, cols]
        total = end + steps_ref[0, n, :, cols] * carry
        for k, by in enumerate((1, 2, 4)):
            total = total + steps_ref[k + 1, n, :, cols] * pltpu.roll(total, by, 0)
        starts_ref[n, :, cols] = jnp.where(head, carry, pltpu.roll(total, 1, 0))
        last[n, :, cols] = jnp.broadcast_to(total[7:8], (8, lanes))


def filter_kernel(count_rows, *refs):
    row_refs, refs = refs[:count_rows], refs[count_rows:]
    filt_ref, rim_in, carry_in, gate_ref, f_ref, g_ref, spectrum_ref, a_ref, mode_ref, skip_ref, steps_ref = refs[:11]
    y_ref, starts_ref, rim_out, carry_out, pad, z_ref, u_ref = refs[-7:]
    count = y_ref.shape[0]
    groups = count // span
    for s in range(3):
        first = 0
        for ref in row_refs:
            place_rows(s, first, ref[s], pad)
            first += ref.shape[1]
        lead_in_all(s, count, pad, rim_in)
        rim_out[s * rim : (s + 1) * rim, :] = row_refs[-1][s, row_refs[-1].shape[1] - rim :, :]
    z_ref[0:span, :] = rim_in[3 * rim :, :]
    for k in range(groups):
        product = featured(pad, filt_ref, 1, k) * featured(pad, filt_ref, 2, k)
        z_ref[span + k * span : 2 * span + k * span, :] = product.astype(jnp.bfloat16)
    rim_out[3 * rim :, :] = z_ref[count : count + span, :]
    for k in range(groups):
        rows = slice(k * span, k * span + span)
        medium = medium_block(z_ref[k * span : k * span + 2 * span, :], f_ref, g_ref, spectrum_ref)
        mixed = (featured(pad, filt_ref, 0, k) * medium).astype(jnp.bfloat16)
        u = gate_ref[rows, :].astype(jnp.float32) * mixed.astype(jnp.float32)
        u_ref[rows, :] = u.astype(jnp.bfloat16).astype(jnp.float32)
    for k in range(groups):
        for lane in range(y_ref.shape[1] // lanes):
            cols = slice(lane * lanes, (lane + 1) * lanes)
            state = recur(k, cols, u_ref, y_ref, a_ref, mode_ref, skip_ref)
            chain(state, cols, carry_in if k == 0 else carry_out, starts_ref.at[k], steps_ref, carry_out)


def run_filters(rows, filt, rim_rows, carry, gate, tables, ties):
    width = rows[0].shape[2]
    count = sum(r.shape[1] for r in rows)
    modes = carry.shape[0]
    operands = [*rows, filt, rim_rows, carry, gate, *tables]
    outs = [
        jax.ShapeDtypeStruct((count, width), jnp.float32),
        jax.ShapeDtypeStruct((count // span, modes, 8, width), jnp.float32),
        jax.ShapeDtypeStruct((3 * rim + span, width), jnp.bfloat16),
        jax.ShapeDtypeStruct((modes, 8, width), jnp.float32),
    ]
    scratch = [
        pltpu.VMEM((3, groups_rows(count), width), jnp.float32),
        pltpu.VMEM((span + count, width), jnp.bfloat16),
        pltpu.VMEM((count, width), jnp.float32),
    ]
    return pl.pallas_call(
        functools.partial(filter_kernel, len(rows)),
        in_specs=[in_vmem] * len(operands) + [in_hbm] * len(ties),
        out_specs=[in_vmem] * 4,
        out_shape=outs,
        scratch_shapes=scratch,
        compiler_params=params(operands, outs, scratch),
        name="filters",
    )(*operands, *ties)


def groups_rows(count):
    return (count // span) * (rim + span)


def project_kernel(layout, count_x, part, *refs):
    order_ref, w_ref, inv_ref, rows_ref, total = refs[count_x:]
    size = rows_of(part)
    for step in project_steps(size, bind(layout, refs[:count_x]), order_ref, w_ref, total):
        step()
    for s in range(3):
        rows_ref[s] = (total[s] * scale_of(inv_ref, *part[0])).astype(jnp.bfloat16)


def project(gathered, order, w, inv, part):
    layout, arrays = gathered
    width, size = w.shape[2], rows_of(part)
    operands = [*arrays, order, w, inv]
    out = jax.ShapeDtypeStruct((3, size, width), jnp.bfloat16)
    scratch = [pltpu.VMEM((3, size, width), jnp.float32)]
    return pl.pallas_call(
        functools.partial(project_kernel, layout, len(arrays), part),
        in_specs=[in_vmem] * len(arrays) + [in_smem] + [in_vmem] * 2,
        out_specs=in_vmem,
        out_shape=out,
        scratch_shapes=scratch,
        compiler_params=params(operands, [out], scratch),
        name="project",
    )(*operands)


def tables_kernel(tokens, decay_ref, weight_ref, skip_ref, taps_ref, shuffle_ref, f_ref, *outs):
    spectrum, decays, weights, skips, steps, run_steps, group_steps, block_steps = outs
    modes, width = decay_ref.shape
    ordered = dot(shuffle_ref[...], taps_ref[...]).astype(jnp.bfloat16)
    both = dot(f_ref[:, 0:span], ordered)
    spec = both[: 2 * span] + both[2 * span :]
    spectrum[0] = spec[:span]
    spectrum[1] = spec[span:]
    skips[...] = jnp.broadcast_to(skip_ref[...], (8, width))
    place = lax.broadcasted_iota(jnp.int32, (8, width), 0)
    for n in range(modes):
        rate = -jnp.broadcast_to(decay_ref[n : n + 1, :], (8, width))
        decays[n] = jnp.exp(rate)
        weights[n] = jnp.broadcast_to(weight_ref[n : n + 1, :], (8, width))
        steps[0, n] = jnp.where(place == 0, jnp.exp(rate * run), 0.0)
        for k, by in enumerate((1, 2, 4)):
            steps[k + 1, n] = jnp.where(place >= by, jnp.exp(rate * (run * by)), 0.0)
        run_steps[n] = jnp.exp(rate * (place * run).astype(jnp.float32))
        group_steps[n] = jnp.exp(rate * span)
    for k in range(block_steps.shape[0]):
        block_steps[k] = jnp.exp(-decay_ref[...] * float(tokens * k))


def mode_tables(decay_rate, residue, skip_gain, mr_filter, shuffler, forward, tokens, blocks):
    modes, width = decay_rate.shape
    weighted = residue * jnp.sqrt(-jnp.expm1(-2.0 * decay_rate))
    wide = jax.ShapeDtypeStruct((modes, 8, width), jnp.float32)
    outs = [
        jax.ShapeDtypeStruct((2, span, width), jnp.float32),
        wide,
        wide,
        jax.ShapeDtypeStruct((8, width), jnp.float32),
        jax.ShapeDtypeStruct((4, modes, 8, width), jnp.float32),
        wide,
        wide,
        jax.ShapeDtypeStruct((blocks, modes, width), jnp.float32),
    ]
    operands = [decay_rate, weighted, skip_gain[None], mr_filter, shuffler, forward]
    return pl.pallas_call(
        functools.partial(tables_kernel, tokens),
        out_shape=outs,
        compiler_params=params(operands, outs),
        name="mode_tables",
    )(*operands)


def finish_kernel(peers, counts, *refs):
    recv, refs = refs[:peers], refs[peers:]
    y_refs, refs = refs[: len(counts)], refs[len(counts) :]
    s_refs, refs = refs[: len(counts)], refs[len(counts) :]
    gate_ref, back_ref, a_ref, mode_ref, skip_runs, skip_group, skip_block, out_hbm, incoming, out_buf, out_ref, sems = refs
    modes = a_ref.shape[0]
    width = out_ref.shape[1]
    for n in range(modes):
        total = jnp.zeros((1, width), jnp.float32)
        for k in range(peers):
            total = total + skip_block[k, n : n + 1, :] * recv[k][n : n + 1, :]
        incoming[n] = jnp.broadcast_to(total, (8, width))

    first = 0
    copies = []
    for y_ref, s_ref, count in zip(y_refs, s_refs, counts):
        def one(k, _, y_ref=y_ref, s_ref=s_ref, first=first):
            base = pl.multiple_of(k * span, span)
            here = pl.multiple_of(first + k * span, span)
            for lane in range(width // lanes):
                cols = slice(lane * lanes, (lane + 1) * lanes)
                a = [a_ref[n, :, cols] for n in range(modes)]
                state = []
                for n in range(modes):
                    coming = incoming[n, :, cols]
                    state.append(mode_ref[n, :, cols] * (s_ref[k, n, :, cols] + skip_runs[n, :, cols] * coming))
                    incoming[n, :, cols] = coming * skip_group[n, :, cols]
                for t in range(run):
                    state = [s * d for s, d in zip(state, a)]
                    out_buf[8 * t : 8 * t + 8, cols] = add_up(state + [y_ref[pl.ds(base + 8 * t, 8), cols]])
            rows = pl.ds(here, span)
            mixed = (out_buf[...] * gate_ref[rows, :].astype(jnp.float32)).astype(jnp.bfloat16)
            out_ref[rows, :] = dot(back_ref[...], mixed).astype(jnp.bfloat16)
            return 0

        lax.fori_loop(0, count, one, 0, unroll=2)
        rows = pl.ds(first, count * span)
        copies.append(pltpu.make_async_copy(out_ref.at[rows, :], out_hbm.at[rows, :], sems.at[len(copies)]))
        copies[-1].start()
        first += count * span
    for copy in copies:
        copy.wait()


def finish(recv, ys, starts, gate, tables):
    tokens, width = gate.shape
    modes = starts[0].shape[1]
    counts = [s.shape[0] for s in starts]
    operands = [*recv, *ys, *starts, gate, *tables]
    out = jax.ShapeDtypeStruct((tokens, width), jnp.bfloat16)
    scratch = [
        pltpu.VMEM((modes, 8, width), jnp.float32),
        pltpu.VMEM((span, width), jnp.float32),
        pltpu.VMEM((tokens, width), jnp.bfloat16),
    ]
    return pl.pallas_call(
        functools.partial(finish_kernel, len(recv), counts),
        in_specs=[in_vmem] * len(operands),
        out_specs=in_hbm,
        out_shape=out,
        scratch_shapes=scratch + [pltpu.SemaphoreType.DMA((len(counts),))],
        compiler_params=params(operands, [], scratch),
        name="finish",
    )(*operands)


def flipped(value, mask, name):
    peers = lax.axis_size("chan")
    with jax.named_scope(name):
        return lax.ppermute(value, "chan", [(i, i ^ mask) for i in range(peers)])


def shifted(value, by, name):
    peers = lax.axis_size("seq")
    with jax.named_scope(name):
        return lax.ppermute(value, "seq", [(i, i + by) for i in range(peers - by)])


def after(value, *others):
    return lax.optimization_barrier((value, *others))[0]


def on_device(
    resid, norm_gain, feat_weight, short_filter, mr_filter, gates_lr, decay_rate, residue, skip_gain
):
    tokens, width = resid.shape
    modes = decay_rate.shape[0]
    parts = parts_of(tokens)
    count = len(parts)
    peers, seq_peers = lax.axis_size("chan"), lax.axis_size("seq")
    square = peers == 8
    me = lax.axis_index("chan")
    order = jnp.arange(peers, dtype=jnp.int32)
    if square:
        order = me ^ order
    weight = feat_weight.transpose(1, 0, 2)
    shuffler = jnp.asarray(shuffle())
    forward, inverse = (jnp.asarray(t) for t in transforms())
    every, *sent = prepare(resid, norm_gain, shuffler, parts)
    bases = [sum(v.shape[0] for v in sent[:i]) for i in range(count)]

    spans = [parts[0][1], parts[1][0], (parts[2][0][0], rows_of(parts[2]) + parts[0][0][1])]
    gate_out, *gate_in = shuffle_gates(gates_lr, [start for start, _ in spans], [size for _, size in spans])
    spectrum, decays, weights, skips, steps, run_steps, group_steps, block_steps = mode_tables(
        decay_rate, residue, skip_gain, mr_filter, shuffler, forward, tokens, max(seq_peers - 1, 1)
    )
    tables = [forward, inverse, spectrum, decays, weights, skips, steps]

    near, far, kept = [None] * count, [None] * count, [None] * count

    def send_near(c, *ties):
        own = after(sent[c], *ties) if ties else sent[c]
        near[c] = flipped(own, 2, f"near_x_{c}"), flipped(own, 4, f"near_y_{c}")

    def send_far(c, *ties):
        half = -(-sent[c].shape[0] // 32) * 16
        x, y = near[c] = tuple(after(v, *ties) for v in near[c])
        far[c] = flipped(x[:half], 4, f"far_x_{c}"), flipped(y[half:], 2, f"far_y_{c}")

    def gathered(c):
        own = sent[c]
        rows = own.shape[0]
        if not square:
            whole_chunk = lax.all_gather(own, "chan")
            arrays = [whole_chunk[i] for i in range(peers)]
            return [[(i, 0, 0, rows)] for i in range(peers)], arrays
        (x, y), (fx, fy) = near[c], far[c]
        twin = [flipped(v, 1, f"{n}_{c}") for v, n in ((x, "twin_x"), (y, "twin_y"), (fx, "twin_fx"), (fy, "twin_fy"))]
        half = fx.shape[0]
        arrays = [own, twin_all, x, twin[0], y, twin[1], fx, fy, twin[2], twin[3]]
        layout = [[(0, 0, 0, rows)], [(1, bases[c], 0, rows)]]
        layout += [[(i, 0, 0, rows)] for i in (2, 3, 4, 5)]
        layout += [[(i, 0, 0, half), (i + 1, 0, half, rows - half)] for i in (6, 8)]
        return layout, arrays

    size = rows_of(parts[0])
    if square:
        send_near(0)
        twin_all = flipped(every, 1, "twin_all")
        begun = begin(every, twin_all, order, weight, bases[:1], [size])[0]
        send_far(0, begun, spectrum, gate_out)
        send_near(1, *near[0])
    else:
        twins = lax.all_gather(every, "chan")
        begun = begin(twins[0], twins[1], order, weight, bases[:1], [size])[0]
    tail_rows_done, rows, rim_rows, inv = project_first(
        gathered(0), order, weight, begun, short_filter, parts[0], tokens
    )
    rim_rows = shifted(rim_rows, 1, "rim")
    carry = jnp.zeros((modes, 8, width), jnp.float32)
    ys, starts = [], []
    for c in range(count):
        if c:
            rows = project(gathered(c), order, weight, inv, parts[c])
            if square and c + 1 < count:
                send_far(c + 1, rows)
        done = [rows] + ([tail_rows_done] if c == count - 1 else [])
        ties = list(near[c + 1]) if square and 0 < c < count - 1 else []
        y, ends, rim_rows, carry = run_filters(done, short_filter, rim_rows, carry, gate_in[c], tables, ties)
        if square and c == 0:
            send_far(1, rim_rows)
            send_near(2, *near[1])
        ys.append(y)
        starts.append(ends)
    end = carry[:, 0, :]
    recv = [shifted(end, by, f"state_{by}") for by in range(1, seq_peers)]
    back = jnp.asarray(shuffle().T)
    finish_tables = [back, decays, weights, run_steps, group_steps, block_steps]
    return finish(recv, ys, starts, gate_out, finish_tables)


def solution(mesh):
    in_specs = (
        P("seq", "chan"),
        P("chan"),
        P(None, None, "chan"),
        P(None, None, "chan"),
        P(None, "chan"),
        P("seq", None, "chan"),
        P(None, "chan"),
        P(None, "chan"),
        P("chan"),
    )
    out_specs = P("seq", "chan")
    return jax.shard_map(
        on_device, mesh=mesh, in_specs=in_specs, out_specs=out_specs, check_vma=False
    )
```

```python
import functools
import math
import jax
import jax.numpy as jnp
import ml_dtypes
import numpy as np
from jax import lax
from jax.experimental import pallas as pl
from jax.experimental.pallas import tpu as pltpu
from jax.sharding import PartitionSpec as P

D = 4096
norm_epsilon = 1e-05
span = 128
run = span // 8
tail_rows = 256
lanes = 128
rim = 16


def split_pair(value):
    high = value.astype(ml_dtypes.bfloat16)
    return high, (value - high.astype(np.float64)).astype(ml_dtypes.bfloat16)


def token_of_row():
    row = np.arange(span)
    return run * (row % 8) + row // 8


def shuffle():
    return np.eye(span)[token_of_row()].astype(ml_dtypes.bfloat16)


def transforms():
    size = 2 * span
    order = token_of_row()
    times = np.concatenate([order, span + order])
    angle = np.pi * (2.0 * np.arange(span)[:, None] + 1.0) * times[None] / size
    forward = np.concatenate([np.cos(angle), -np.sin(angle)], axis=0)
    inverse = np.concatenate([np.cos(angle).T, -np.sin(angle).T], axis=1)[span:] / span
    f_hi, f_lo = split_pair(forward)
    g_hi, g_lo = split_pair(inverse)
    return np.concatenate([f_hi, f_lo], axis=0), np.concatenate([g_hi, g_lo], axis=0)


def dot(a, b):
    return jnp.dot(a, b, preferred_element_type=jnp.float32)


def parts_of(tokens):
    tail, first = 2 * span, 3 * span
    rest = tokens - tail - first
    second = -(-rest // (2 * span)) * span
    return [
        [(tokens - tail, tail), (0, first)],
        [(first, second)],
        [(first + second, rest - second)],
    ]


def rows_of(part):
    return sum(size for _, size in part)


def stat_rows_of(tokens, width):
    return -(-3 * (tokens // width) // 16) * 16


def prepare_kernel(parts, resid_ref, gain_ref, shuffle_ref, all_ref, *outs):
    tokens, width = resid_ref.shape
    ones = jnp.ones((8, width), jnp.bfloat16)
    gain = gain_ref[...].astype(jnp.float32)
    contract = (((1,), (1,)), ((), ()))
    sums = []
    base = 0
    for out, part in zip(outs, parts):
        here = 0
        for start, size in part:
            for at in range(start, start + size, span):
                values = dot(shuffle_ref[...], resid_ref[at : at + span, :])
                scaled = (values * gain).astype(jnp.bfloat16)
                out[here : here + span, :] = scaled
                all_ref[base + here : base + here + span, :] = scaled
                here += span
                square = values * values
                high = square.astype(jnp.bfloat16)
                low = (square - high.astype(jnp.float32)).astype(jnp.bfloat16)
                total = lax.dot_general(ones, high, contract, preferred_element_type=jnp.float32)
                total = total + lax.dot_general(ones, low, contract, preferred_element_type=jnp.float32)
                sums.append((at, total[0:1]))
        base += out.shape[0]
    sums = jnp.concatenate([total for _, total in sorted(sums, key=lambda pair: pair[0])], axis=1)
    count = tokens // width
    rest = jnp.concatenate([sums[:, k * width : (k + 1) * width] for k in range(count)], axis=0)
    shares = []
    for _ in range(3):
        share = rest.astype(jnp.bfloat16)
        rest = rest - share.astype(jnp.float32)
        shares.append(share.astype(jnp.float32))
    spare = stat_rows_of(tokens, width) - 3 * count
    if spare:
        shares.append(jnp.zeros((spare, width), jnp.float32))
    stats = jnp.concatenate(shares, axis=0).astype(jnp.bfloat16)
    first = rows_of(parts[0])
    outs[0][first:, :] = stats
    all_ref[first : first + stats.shape[0], :] = stats


def prepare(resid, norm_gain, shuffler, parts):
    tokens, width = resid.shape
    extra = stat_rows_of(tokens, width)
    shapes = [jax.ShapeDtypeStruct((tokens + extra, width), jnp.bfloat16)]
    for i, part in enumerate(parts):
        shapes.append(jax.ShapeDtypeStruct((rows_of(part) + (extra if i == 0 else 0), width), jnp.bfloat16))
    return pl.pallas_call(
        functools.partial(prepare_kernel, parts),
        out_shape=shapes,
        compiler_params=params([resid, shuffler], shapes),
        name="prepare",
    )(resid, norm_gain[None], shuffler)


def gates_kernel(spans, gates_ref, select_ref, out_ref, *in_refs):
    width = out_ref.shape[1]
    for in_ref, first in zip(in_refs, spans):
        for k in range(in_ref.shape[0] // span):
            at = first + k * span
            both = dot(select_ref[...], gates_ref[at : at + span].reshape(2 * span, width))
            out_ref[at : at + span, :] = both[:span].astype(jnp.bfloat16)
            in_ref[k * span : (k + 1) * span, :] = both[span:].astype(jnp.bfloat16)


def shuffle_gates(gates, spans, sizes):
    tokens, _, width = gates.shape
    select = np.zeros((2 * span, 2 * span), np.float32)
    for row, token in enumerate(token_of_row()):
        select[row, 2 * token] = 1.0
        select[span + row, 2 * token + 1] = 1.0
    outs = [jax.ShapeDtypeStruct((size, width), jnp.bfloat16) for size in [tokens, *sizes]]
    return pl.pallas_call(
        functools.partial(gates_kernel, spans),
        in_specs=[in_vmem] * 2,
        out_specs=[in_vmem] * (1 + len(sizes)),
        out_shape=outs,
        compiler_params=params([gates], outs),
        name="shuffle_gates",
    )(gates, jnp.asarray(select, jnp.bfloat16))


def project_stream(s, size, pieces, order_ref, w_ref, total):
    for b, parts in enumerate(pieces):
        for ref, src, dst, rows in parts:
            depth = ref.shape[1]
            at = pl.multiple_of(order_ref[b] * depth, depth)
            rows = min(rows, size - dst)
            part = dot(ref[src : src + rows, :], w_ref[s, pl.ds(at, depth), :])
            if b == 0:
                total[dst : dst + rows, :] = part
            else:
                total[dst : dst + rows, :] += part


def bind(layout, refs):
    return [[(refs[i], src, dst, rows) for i, src, dst, rows in parts] for parts in layout]


def params(operands, outs, scratch=()):
    held = sum(math.prod(a.shape) * a.dtype.itemsize for a in (*operands, *outs))
    held += sum(math.prod(a.shape) * jnp.dtype(a.dtype).itemsize for a in scratch if len(a.shape) > 1)
    return pltpu.CompilerParams(vmem_limit_bytes=held + (2 << 20))


def whole(shape):
    return pl.BlockSpec(shape, lambda i: (0,) * len(shape))


in_vmem = pl.BlockSpec(memory_space=pltpu.VMEM)
in_smem = pl.BlockSpec(memory_space=pltpu.SMEM)
in_hbm = pl.BlockSpec(memory_space=pl.ANY)

def scale_of(inv_ref, start, size):
    width = inv_ref.shape[0]
    pieces, at = [], start
    while at < start + size:
        column, row = divmod(at, width)
        count = min(width - row, start + size - at)
        pieces.append(inv_ref[row : row + count, column : column + 1])
        at += count
    return pieces[0] if len(pieces) == 1 else jnp.concatenate(pieces, axis=0)


def lead_in(s, k, pad, before):
    base = k * (rim + span)
    head = lax.broadcasted_iota(jnp.int32, (8, pad.shape[2]), 0) == 0
    for half in range(2):
        last = pad[s, base + span + 8 * half : base + span + 8 * half + 8, :]
        pad[s, base + 8 * half : base + 8 * half + 8, :] = jnp.where(head, pltpu.roll(before[half], 1, 0), pltpu.roll(last, 1, 0))


def lead_in_all(s, count, pad, rim_ref):
    last = rim_ref[s * rim : (s + 1) * rim, :].astype(jnp.float32)
    before = [last[0:8], last[8:16]]
    for k in range(count // span):
        lead_in(s, k, pad, before)
        end = (k + 1) * (rim + span)
        before = [pad[s, end - 16 : end - 8, :], pad[s, end - 8 : end, :]]


def place_rows(s, first, value, pad):
    for k in range(value.shape[0] // span):
        base = (first // span + k) * (rim + span) + rim
        pad[s, base : base + span, :] = value[k * span : (k + 1) * span].astype(jnp.float32)


def featured(pad, filt_ref, s, k):
    base = k * (rim + span)
    out = pad[s, base + 16 : base + 16 + span, :] * filt_ref[0, s : s + 1, :]
    out = out + pad[s, base + 8 : base + 8 + span, :] * filt_ref[1, s : s + 1, :]
    return out + pad[s, base : base + span, :] * filt_ref[2, s : s + 1, :]


def first_kernel(layout, count_x, part, tokens, *refs):
    x_refs, refs = refs[:count_x], refs[count_x:]
    order_ref, w_ref, filt_ref, tail_ref, rows_ref, rim_ref, inv_ref, pad, total = refs
    size, tail, width = rows_of(part), tail_ref.shape[1], inv_ref.shape[0]
    pieces = bind(layout, x_refs)
    count = tokens // width
    stat_count = stat_rows_of(tokens, width)
    sums = jnp.zeros((count, width), jnp.float32)
    for parts in pieces:
        ref, src, dst, rows = parts[-1]
        stats = ref[src + size - dst : src + size - dst + stat_count, :].astype(jnp.float32)
        for k in range(3):
            sums = sums + stats[k * count : (k + 1) * count]
    inverse = lax.rsqrt(sums / D + norm_epsilon)
    if count < 8:
        inverse = jnp.concatenate([inverse, jnp.zeros((8 - count, width), jnp.float32)], axis=0)
    inv_ref[...] = inverse.T
    end = (tail // span) * (rim + span)
    for s in range(3):
        project_stream(s, size, pieces, order_ref, w_ref, total)
        tail_ref[s] = (total[0:tail, :] * scale_of(inv_ref, *part[0])).astype(jnp.bfloat16)
        rows_ref[s] = (total[tail:, :] * scale_of(inv_ref, *part[1])).astype(jnp.bfloat16)
        place_rows(s, 0, tail_ref[s], pad)
        rim_ref[s * rim : (s + 1) * rim, :] = tail_ref[s, tail - rim :, :]
        lead_in_all(s, tail, pad, rim_ref)
    last = tail // span - 1
    product = featured(pad, filt_ref, 1, last) * featured(pad, filt_ref, 2, last)
    rim_ref[3 * rim :, :] = product.astype(jnp.bfloat16)


def project_first(gathered, order, w, filt, part, tokens):
    layout, arrays = gathered
    width = w.shape[2]
    (_, tail), (_, size) = part
    operands = [*arrays, order, w, filt]
    outs = [
        jax.ShapeDtypeStruct((3, tail, width), jnp.bfloat16),
        jax.ShapeDtypeStruct((3, size, width), jnp.bfloat16),
        jax.ShapeDtypeStruct((3 * rim + span, width), jnp.bfloat16),
        jax.ShapeDtypeStruct((width, 8), jnp.float32),
    ]
    scratch = [
        pltpu.VMEM((3, groups_rows(tail), width), jnp.float32),
        pltpu.VMEM((tail + size, width), jnp.float32),
    ]
    return pl.pallas_call(
        functools.partial(first_kernel, layout, len(arrays), part, tokens),
        in_specs=[in_vmem] * len(arrays) + [in_smem] + [in_vmem] * 2,
        out_specs=[in_vmem] * 4,
        out_shape=outs,
        scratch_shapes=scratch,
        compiler_params=params([*arrays, w, filt], outs, scratch),
        name="project_first",
    )(*operands)


def medium_block(window, f_ref, g_ref, spectrum_ref):
    both = dot(f_ref[...], window)
    spec = both[: 2 * span] + both[2 * span :]
    real, imag = spec[:span], spec[span:]
    h_real, h_imag = spectrum_ref[0], spectrum_ref[1]
    out = jnp.concatenate([real * h_real - imag * h_imag, real * h_imag + imag * h_real], axis=0)
    high = out.astype(jnp.bfloat16)
    low = (out - high.astype(jnp.float32)).astype(jnp.bfloat16)
    pair = dot(g_ref[...], high)
    return pair[:span] + pair[span:] + dot(g_ref[0:span, :], low)


def add_up(terms):
    while len(terms) > 1:
        paired = [terms[i] + terms[i + 1] for i in range(0, len(terms) - 1, 2)]
        terms = paired + terms[len(terms) - len(terms) % 2 :]
    return terms[0]


def recur(k, cols, u_ref, y_ref, a_ref, w_ref, skip_ref):
    modes = a_ref.shape[0]
    a = [a_ref[n, :, cols] for n in range(modes)]
    w = [w_ref[n, :, cols] for n in range(modes)]
    skip = skip_ref[:, cols]
    state = [None] * modes
    for t in range(run):
        rows = slice(k * span + 8 * t, k * span + 8 * t + 8)
        u = u_ref[rows, cols]
        state = [u if t == 0 else s * d + u for s, d in zip(state, a)]
        y_ref[rows, cols] = add_up([s * v for s, v in zip(state, w)] + [skip * u])
    return state


def chain(state, cols, carry_ref, starts_ref, steps_ref, last):
    head = lax.broadcasted_iota(jnp.int32, (8, lanes), 0) == 0
    for n, end in enumerate(state):
        carry = carry_ref[n, :, cols]
        total = end + steps_ref[0, n, :, cols] * carry
        for k, by in enumerate((1, 2, 4)):
            total = total + steps_ref[k + 1, n, :, cols] * pltpu.roll(total, by, 0)
        starts_ref[n, :, cols] = jnp.where(head, carry, pltpu.roll(total, 1, 0))
        last[n, :, cols] = jnp.broadcast_to(total[7:8], (8, lanes))


def filter_kernel(count_rows, *refs):
    row_refs, refs = refs[:count_rows], refs[count_rows:]
    filt_ref, rim_in, carry_in, gate_ref, f_ref, g_ref, spectrum_ref, a_ref, mode_ref, skip_ref, steps_ref = refs[:11]
    y_ref, starts_ref, rim_out, carry_out, pad, z_ref, u_ref = refs[-7:]
    count = y_ref.shape[0]
    groups = count // span
    for s in range(3):
        first = 0
        for ref in row_refs:
            place_rows(s, first, ref[s], pad)
            first += ref.shape[1]
        lead_in_all(s, count, pad, rim_in)
        rim_out[s * rim : (s + 1) * rim, :] = row_refs[-1][s, row_refs[-1].shape[1] - rim :, :]
    z_ref[0:span, :] = rim_in[3 * rim :, :]
    for k in range(groups):
        product = featured(pad, filt_ref, 1, k) * featured(pad, filt_ref, 2, k)
        z_ref[span + k * span : 2 * span + k * span, :] = product.astype(jnp.bfloat16)
    rim_out[3 * rim :, :] = z_ref[count : count + span, :]
    for k in range(groups):
        rows = slice(k * span, k * span + span)
        medium = medium_block(z_ref[k * span : k * span + 2 * span, :], f_ref, g_ref, spectrum_ref)
        mixed = (featured(pad, filt_ref, 0, k) * medium).astype(jnp.bfloat16)
        u = gate_ref[rows, :].astype(jnp.float32) * mixed.astype(jnp.float32)
        u_ref[rows, :] = u.astype(jnp.bfloat16).astype(jnp.float32)
    for k in range(groups):
        for lane in range(y_ref.shape[1] // lanes):
            cols = slice(lane * lanes, (lane + 1) * lanes)
            state = recur(k, cols, u_ref, y_ref, a_ref, mode_ref, skip_ref)
            chain(state, cols, carry_in if k == 0 else carry_out, starts_ref.at[k], steps_ref, carry_out)


def run_filters(rows, filt, rim_rows, carry, gate, tables, ties):
    width = rows[0].shape[2]
    count = sum(r.shape[1] for r in rows)
    modes = carry.shape[0]
    operands = [*rows, filt, rim_rows, carry, gate, *tables]
    outs = [
        jax.ShapeDtypeStruct((count, width), jnp.float32),
        jax.ShapeDtypeStruct((count // span, modes, 8, width), jnp.float32),
        jax.ShapeDtypeStruct((3 * rim + span, width), jnp.bfloat16),
        jax.ShapeDtypeStruct((modes, 8, width), jnp.float32),
    ]
    scratch = [
        pltpu.VMEM((3, groups_rows(count), width), jnp.float32),
        pltpu.VMEM((span + count, width), jnp.bfloat16),
        pltpu.VMEM((count, width), jnp.float32),
    ]
    return pl.pallas_call(
        functools.partial(filter_kernel, len(rows)),
        in_specs=[in_vmem] * len(operands) + [in_hbm] * len(ties),
        out_specs=[in_vmem] * 4,
        out_shape=outs,
        scratch_shapes=scratch,
        compiler_params=params(operands, outs, scratch),
        name="filters",
    )(*operands, *ties)


def groups_rows(count):
    return (count // span) * (rim + span)


def project_kernel(layout, count_x, part, *refs):
    order_ref, w_ref, inv_ref, rows_ref, total = refs[count_x:]
    size = rows_of(part)
    for s in range(3):
        project_stream(s, size, bind(layout, refs[:count_x]), order_ref, w_ref, total)
        rows_ref[s] = (total[...] * scale_of(inv_ref, *part[0])).astype(jnp.bfloat16)


def project(gathered, order, w, inv, part):
    layout, arrays = gathered
    width, size = w.shape[2], rows_of(part)
    operands = [*arrays, order, w, inv]
    out = jax.ShapeDtypeStruct((3, size, width), jnp.bfloat16)
    scratch = [pltpu.VMEM((size, width), jnp.float32)]
    return pl.pallas_call(
        functools.partial(project_kernel, layout, len(arrays), part),
        in_specs=[in_vmem] * len(arrays) + [in_smem] + [in_vmem] * 2,
        out_specs=in_vmem,
        out_shape=out,
        scratch_shapes=scratch,
        compiler_params=params([*arrays, w, inv], [out], scratch),
        name="project",
    )(*operands)


def tables_kernel(tokens, decay_ref, weight_ref, skip_ref, taps_ref, shuffle_ref, f_ref, *outs):
    spectrum, decays, weights, skips, steps, run_steps, group_steps, block_steps = outs
    modes, width = decay_ref.shape
    ordered = dot(shuffle_ref[...], taps_ref[...]).astype(jnp.bfloat16)
    both = dot(f_ref[:, 0:span], ordered)
    spec = both[: 2 * span] + both[2 * span :]
    spectrum[0] = spec[:span]
    spectrum[1] = spec[span:]
    skips[...] = jnp.broadcast_to(skip_ref[...], (8, width))
    place = lax.broadcasted_iota(jnp.int32, (8, width), 0)
    for n in range(modes):
        rate = -jnp.broadcast_to(decay_ref[n : n + 1, :], (8, width))
        decays[n] = jnp.exp(rate)
        weights[n] = jnp.broadcast_to(weight_ref[n : n + 1, :], (8, width))
        steps[0, n] = jnp.where(place == 0, jnp.exp(rate * run), 0.0)
        for k, by in enumerate((1, 2, 4)):
            steps[k + 1, n] = jnp.where(place >= by, jnp.exp(rate * (run * by)), 0.0)
        run_steps[n] = jnp.exp(rate * (place * run).astype(jnp.float32))
        group_steps[n] = jnp.exp(rate * span)
    for k in range(block_steps.shape[0]):
        block_steps[k] = jnp.exp(-decay_ref[...] * float(tokens * k))


def mode_tables(decay_rate, residue, skip_gain, mr_filter, shuffler, forward, tokens, blocks):
    modes, width = decay_rate.shape
    weighted = residue * jnp.sqrt(-jnp.expm1(-2.0 * decay_rate))
    wide = jax.ShapeDtypeStruct((modes, 8, width), jnp.float32)
    outs = [
        jax.ShapeDtypeStruct((2, span, width), jnp.float32),
        wide,
        wide,
        jax.ShapeDtypeStruct((8, width), jnp.float32),
        jax.ShapeDtypeStruct((4, modes, 8, width), jnp.float32),
        wide,
        wide,
        jax.ShapeDtypeStruct((blocks, modes, width), jnp.float32),
    ]
    operands = [decay_rate, weighted, skip_gain[None], mr_filter, shuffler, forward]
    return pl.pallas_call(
        functools.partial(tables_kernel, tokens),
        out_shape=outs,
        compiler_params=params(operands, outs),
        name="mode_tables",
    )(*operands)


def finish_kernel(peers, counts, *refs):
    recv, refs = refs[:peers], refs[peers:]
    y_refs, refs = refs[: len(counts)], refs[len(counts) :]
    s_refs, refs = refs[: len(counts)], refs[len(counts) :]
    gate_ref, back_ref, a_ref, mode_ref, skip_runs, skip_group, skip_block, out_hbm, incoming, out_buf, out_ref, sems = refs
    modes = a_ref.shape[0]
    width = out_ref.shape[1]
    for n in range(modes):
        total = jnp.zeros((1, width), jnp.float32)
        for k in range(peers):
            total = total + skip_block[k, n : n + 1, :] * recv[k][n : n + 1, :]
        incoming[n] = jnp.broadcast_to(total, (8, width))

    first = 0
    copies = []
    for y_ref, s_ref, count in zip(y_refs, s_refs, counts):
        def one(k, _, y_ref=y_ref, s_ref=s_ref, first=first):
            base = pl.multiple_of(k * span, span)
            here = pl.multiple_of(first + k * span, span)
            for lane in range(width // lanes):
                cols = slice(lane * lanes, (lane + 1) * lanes)
                a = [a_ref[n, :, cols] for n in range(modes)]
                state = []
                for n in range(modes):
                    coming = incoming[n, :, cols]
                    state.append(mode_ref[n, :, cols] * (s_ref[k, n, :, cols] + skip_runs[n, :, cols] * coming))
                    incoming[n, :, cols] = coming * skip_group[n, :, cols]
                for t in range(run):
                    state = [s * d for s, d in zip(state, a)]
                    out_buf[8 * t : 8 * t + 8, cols] = add_up(state + [y_ref[pl.ds(base + 8 * t, 8), cols]])
            rows = pl.ds(here, span)
            mixed = (out_buf[...] * gate_ref[rows, :].astype(jnp.float32)).astype(jnp.bfloat16)
            out_ref[rows, :] = dot(back_ref[...], mixed).astype(jnp.bfloat16)
            return 0

        lax.fori_loop(0, count, one, 0, unroll=2)
        rows = pl.ds(first, count * span)
        copies.append(pltpu.make_async_copy(out_ref.at[rows, :], out_hbm.at[rows, :], sems.at[len(copies)]))
        copies[-1].start()
        first += count * span
    for copy in copies:
        copy.wait()


def finish(recv, ys, starts, gate, tables):
    tokens, width = gate.shape
    modes = starts[0].shape[1]
    counts = [s.shape[0] for s in starts]
    operands = [*recv, *ys, *starts, gate, *tables]
    out = jax.ShapeDtypeStruct((tokens, width), jnp.bfloat16)
    scratch = [
        pltpu.VMEM((modes, 8, width), jnp.float32),
        pltpu.VMEM((span, width), jnp.float32),
        pltpu.VMEM((tokens, width), jnp.bfloat16),
    ]
    return pl.pallas_call(
        functools.partial(finish_kernel, len(recv), counts),
        in_specs=[in_vmem] * len(operands),
        out_specs=in_hbm,
        out_shape=out,
        scratch_shapes=scratch + [pltpu.SemaphoreType.DMA((len(counts),))],
        compiler_params=params(operands, [], scratch),
        name="finish",
    )(*operands)


def flipped(value, mask, name):
    peers = lax.axis_size("chan")
    with jax.named_scope(name):
        return lax.ppermute(value, "chan", [(i, i ^ mask) for i in range(peers)])


def shifted(value, by, name):
    peers = lax.axis_size("seq")
    with jax.named_scope(name):
        return lax.ppermute(value, "seq", [(i, i + by) for i in range(peers - by)])


def after(value, *others):
    return lax.optimization_barrier((value, *others))[0]


def on_device(
    resid, norm_gain, feat_weight, short_filter, mr_filter, gates_lr, decay_rate, residue, skip_gain
):
    tokens, width = resid.shape
    modes = decay_rate.shape[0]
    parts = parts_of(tokens)
    count = len(parts)
    peers, seq_peers = lax.axis_size("chan"), lax.axis_size("seq")
    square = peers == 8
    me = lax.axis_index("chan")
    order = jnp.arange(peers, dtype=jnp.int32)
    if square:
        order = me ^ order
    weight = feat_weight.transpose(1, 0, 2)
    shuffler = jnp.asarray(shuffle())
    forward, inverse = (jnp.asarray(t) for t in transforms())
    every, *sent = prepare(resid, norm_gain, shuffler, parts)
    bases = [sum(v.shape[0] for v in sent[:i]) for i in range(count)]

    spans = [parts[0][1], parts[1][0], (parts[2][0][0], rows_of(parts[2]) + parts[0][0][1])]
    gate_out, *gate_in = shuffle_gates(gates_lr, [start for start, _ in spans], [size for _, size in spans])
    spectrum, decays, weights, skips, steps, run_steps, group_steps, block_steps = mode_tables(
        decay_rate, residue, skip_gain, mr_filter, shuffler, forward, tokens, max(seq_peers - 1, 1)
    )
    tables = [forward, inverse, spectrum, decays, weights, skips, steps]

    near, far, kept = [None] * count, [None] * count, [None] * count

    def send_near(c, *ties):
        own = after(sent[c], *ties) if ties else sent[c]
        near[c] = flipped(own, 2, f"near_x_{c}"), flipped(own, 4, f"near_y_{c}")

    def send_far(c, *ties):
        half = -(-sent[c].shape[0] // 32) * 16
        x, y = near[c] = tuple(after(v, *ties) for v in near[c])
        far[c] = flipped(x[:half], 4, f"far_x_{c}"), flipped(y[half:], 2, f"far_y_{c}")

    def gathered(c):
        own = sent[c]
        rows = own.shape[0]
        if not square:
            whole_chunk = lax.all_gather(own, "chan")
            arrays = [whole_chunk[i] for i in range(peers)]
            return [[(i, 0, 0, rows)] for i in range(peers)], arrays
        (x, y), (fx, fy) = near[c], far[c]
        twin = [flipped(v, 1, f"{n}_{c}") for v, n in ((x, "twin_x"), (y, "twin_y"), (fx, "twin_fx"), (fy, "twin_fy"))]
        half = fx.shape[0]
        arrays = [own, twin_all, x, twin[0], y, twin[1], fx, fy, twin[2], twin[3]]
        layout = [[(0, 0, 0, rows)], [(1, bases[c], 0, rows)]]
        layout += [[(i, 0, 0, rows)] for i in (2, 3, 4, 5)]
        layout += [[(i, 0, 0, half), (i + 1, 0, half, rows - half)] for i in (6, 8)]
        return layout, arrays

    if square:
        send_near(0)
        twin_all = flipped(every, 1, "twin_all")
        send_far(0, gate_out, spectrum)
        send_near(1, *near[0])
    tail_rows_done, rows, rim_rows, inv = project_first(gathered(0), order, weight, short_filter, parts[0], tokens)
    rim_rows = shifted(rim_rows, 1, "rim")
    if square:
        send_far(1, rows)
        send_near(2, *near[1])
    carry = jnp.zeros((modes, 8, width), jnp.float32)
    ys, starts = [], []
    for c in range(count):
        if c:
            rows = project(gathered(c), order, weight, after(inv, carry), parts[c])
            if square and c + 1 < count:
                send_far(c + 1, rows)
        done = [rows] + ([tail_rows_done] if c == count - 1 else [])
        ties = list(near[c + 1]) if square and 0 < c < count - 1 else []
        y, ends, rim_rows, carry = run_filters(done, short_filter, rim_rows, carry, gate_in[c], tables, ties)
        ys.append(y)
        starts.append(ends)
    end = carry[:, 0, :]
    recv = [shifted(end, by, f"state_{by}") for by in range(1, seq_peers)]
    back = jnp.asarray(shuffle().T)
    finish_tables = [back, decays, weights, run_steps, group_steps, block_steps]
    return finish(recv, ys, starts, gate_out, finish_tables)


def solution(mesh):
    in_specs = (
        P("seq", "chan"),
        P("chan"),
        P(None, None, "chan"),
        P(None, None, "chan"),
        P(None, "chan"),
        P("seq", None, "chan"),
        P(None, "chan"),
        P(None, "chan"),
        P("chan"),
    )
    out_specs = P("seq", "chan")
    return jax.shard_map(
        on_device, mesh=mesh, in_specs=in_specs, out_specs=out_specs, check_vma=False
    )
```
